32 devices in a mesh: space: 8 (over z, y), filt: 4 (over x, core).
Axes of the slice: x: 2, y: 2, z: 4, core: 2. Of those that a mesh axis runs over, the one named last changes fastest.
Arguments:
- features: bfloat16 [128, 128, 1024], P('space', 'filt'), may hold values from -6 to 6
- grad_out: bfloat16 [128, 128, 1024], P('space', 'filt'), may hold values from -6 to 6
- weight: bfloat16 [3, 3, 128, 128], P(None, None, 'filt'), may hold values from -0.1875 to 0.1875
Outputs:
- grad_features: bfloat16 [128, 128, 1024], P('space', 'filt')
- grad_weight: float32 [3, 3, 128, 128], P(None, None, 'filt')
The draws below stay inside these ranges and needn't reach their ends.
All inputs are finite; a program needn't handle non-finite values.
Results may differ from the reference program's by a relative error of at most 0.001.
Values may be sent and summed in bfloat16 or wider, within the bound.
A program may use at most 192 MiB of HBM per device.

```python
import jax
import jax.numpy as jnp
from jax import lax

CIN = 128
COUT = 128
R_DEV = 16
W = 1024
ROWS = 128


def steps_of(stream_key, shape, shards, low, top_value):
    factor_of, own = 1.0, jax.random.fold_in(stream_key, 6)
    for position, shards_of in shards:
        heights = jnp.exp(jax.random.uniform(jax.random.fold_in(own, position), (shards_of,), jnp.float32, low / len(shards), top_value / len(shards)))
        factor_of = factor_of * jnp.repeat(heights, shape[position] // shards_of).reshape([-1 if axis == position else 1 for axis in range(len(shape))])
    return factor_of


def noise(rng, extent, scale, most, split=(), held_as=jnp.bfloat16):
    factor_of = steps_of(rng, extent, split, -0.22, 0.18) if split else 1.0
    array = jax.random.normal(rng, extent, jnp.float32) * scale * factor_of
    return jnp.minimum(jnp.maximum(array, -most), most).astype(held_as)


def setup_inputs(seed: int = 0) -> dict:
    arg_keys = jax.random.split(jax.random.key(seed), 4)
    return {
        "features": noise(arg_keys[0], (ROWS, CIN, W), 1.0, 6.0, ((0, 8), (1, 4))),
        "grad_out": noise(arg_keys[1], (ROWS, COUT, W), 1.0, 6.0, ((0, 8), (1, 4))),
        "weight": noise(arg_keys[2], (3, 3, COUT, CIN), (9 * COUT) ** -0.5, 0.1875, ((2, 4),)),
    }


def reference(features, grad_out, weight):
    width = features.shape[2]
    padded_x = jnp.pad(features, ((1, 1), (0, 0), (1, 1)))
    padded_g = jnp.pad(grad_out, ((1, 1), (0, 0), (1, 1)))
    weight_f = weight.astype(jnp.float32)
    nblocks = ROWS // R_DEV

    def step(acc, index):
        start = (index * R_DEV).astype(jnp.int32)
        xblock = lax.dynamic_slice_in_dim(padded_x, start, R_DEV + 2, 0).astype(jnp.float32)
        gblock = lax.dynamic_slice_in_dim(padded_g, start, R_DEV + 2, 0).astype(jnp.float32)
        center = gblock[1:1 + R_DEV, :, 1:1 + width]
        data = jnp.zeros((R_DEV, CIN, width), jnp.float32)
        for tap_a in range(3):
            for tap_b in range(3):
                shifted = gblock[2 - tap_a:2 - tap_a + R_DEV, :, 2 - tap_b:2 - tap_b + width]
                data = data + jnp.einsum('oc,hox->hcx', weight_f[tap_a, tap_b], shifted)
                window = xblock[tap_a:tap_a + R_DEV, :, tap_b:tap_b + width]
                acc = acc.at[tap_a, tap_b].add(jnp.einsum('hox,hcx->oc', center, window))
        return (acc, data.astype(jnp.bfloat16))
    acc, blocks = lax.scan(step, jnp.zeros((3, 3, COUT, CIN), jnp.float32), jnp.arange(nblocks, dtype=jnp.int32))
    grad_features = blocks.reshape(ROWS, CIN, width)
    grad_weight = acc / jnp.sqrt(jnp.float32(ROWS * width))
    return (grad_features, grad_weight)
```

```python
import functools

import jax
import jax.numpy as jnp
from jax import lax
from jax.experimental import pallas as pl
from jax.experimental.pallas import tpu as pltpu
from jax.sharding import PartitionSpec as P

MESH = pl.DeviceIdType.MESH
NT = (((1,), (1,)), ((), ()))
PIECES = 8


def kernel(n, rows, ch, width, x_ref, g_ref, w_ref, out_ref, gw_ref,
           gall, xraw, xs, wall, wlhs, fs, rs, red,
           loc, sib_s, sib_r, px_s, px_r, fw_s, fw_r, hg_s, hg_r, hx_s, hx_r,
           w_s, w_r, rs_s, rs_r, ag_s, ag_r):
    s = lax.axis_index("space")
    f = lax.axis_index("filt")
    total = 4 * n
    me = s * 4 + f
    sib = f + 1 - 2 * lax.rem(f, 2)
    far = lax.rem(f + 2, 4)
    diag = lax.rem(sib + 2, 4)
    peers = (f, sib, far, diag)
    stride = n // PIECES
    steps = (rows - 2) // 2

    barrier = pltpu.get_barrier_semaphore()

    def greet(i, carry):
        t = lax.rem(me + i, total)
        pl.semaphore_signal(barrier, inc=1, device_id=(t // 4, lax.rem(t, 4)), device_id_type=MESH)
        return carry

    lax.fori_loop(1, total, greet, 0)

    local_g = pltpu.make_async_copy(g_ref, gall.at[pl.ds(1, rows), pl.ds(0, ch)], loc.at[0])
    local_x = pltpu.make_async_copy(x_ref, xraw.at[pl.ds(1, rows)], loc.at[1])
    local_w = pltpu.make_async_copy(w_ref.at[f], wall.at[pl.ds(0, ch)], loc.at[2])
    local_g.start()
    local_x.start()
    local_w.start()
    pl.semaphore_wait(barrier, total - 1)

    def remote(src, dst, ssem, rsem, dev):
        return pltpu.make_async_remote_copy(
            src_ref=src, dst_ref=dst, send_sem=ssem, recv_sem=rsem,
            device_id=dev, device_id_type=MESH)

    def across(first, count, c):
        return remote(g_ref.at[pl.ds(first, count)],
                      gall.at[pl.ds(first + 1, count), pl.ds(2 * ch, ch)],
                      px_s.at[c], px_r.at[c], (s, far))

    def forward(first, count, c):
        return remote(gall.at[pl.ds(first + 1, count), pl.ds(2 * ch, ch)],
                      gall.at[pl.ds(first + 1, count), pl.ds(3 * ch, ch)],
                      fw_s.at[c], fw_r.at[c], (s, sib))

    def edge_rows(k):
        return (0 if k == 0 else rows - 1, 1, k)

    def weights(p):
        return remote(w_ref.at[peers[p]], wall.at[pl.ds(p * ch, ch)], w_s.at[p], w_r.at[p],
                      (s, peers[p]))

    to_sib = remote(g_ref, gall.at[pl.ds(1, rows), pl.ds(ch, ch)], sib_s, sib_r, (s, sib))

    def halo_g(p, d):
        part = pl.ds(p * ch, ch)
        src = gall.at[rows if d == 0 else 1, part] if p else g_ref.at[rows - 1 if d == 0 else 0]
        return remote(src, gall.at[0 if d == 0 else rows + 1, part],
                      hg_s.at[p, d], hg_r.at[p, d], (s + 1 if d == 0 else s - 1, f))

    def halo_x(d):
        return remote(x_ref.at[rows - 1 if d == 0 else 0], xraw.at[0 if d == 0 else rows + 1],
                      hx_s.at[d], hx_r.at[d], (s + 1 if d == 0 else s - 1, f))

    has_next = s < n - 1
    has_prev = s > 0

    def send_halo(p):
        @pl.when(has_next)
        def _():
            halo_g(p, 0).start()

        @pl.when(has_prev)
        def _():
            halo_g(p, 1).start()

    across(*edge_rows(0)).start()
    across(*edge_rows(1)).start()
    for p in (2, 3, 1):
        weights(p).start()

    def start_across(k, carry):
        across(1 + 2 * k, 2, 2 + k).start()
        return carry

    lax.fori_loop(0, steps, start_across, 0)
    to_sib.start()

    @pl.when(has_next)
    def _():
        halo_x(0).start()

    @pl.when(has_prev)
    def _():
        halo_x(1).start()

    send_halo(0)

    @pl.when(jnp.logical_not(has_prev))
    def _():
        gall[0] = jnp.zeros(gall.shape[1:], gall.dtype)
        xraw[0] = jnp.zeros(xraw.shape[1:], xraw.dtype)

    @pl.when(jnp.logical_not(has_next))
    def _():
        gall[rows + 1] = jnp.zeros(gall.shape[1:], gall.dtype)
        xraw[rows + 1] = jnp.zeros(xraw.shape[1:], xraw.dtype)

    lane = lax.broadcasted_iota(jnp.int32, (ch, width), 1)

    def from_left(v):
        return jnp.where(lane == 0, 0.0, pltpu.roll(v, 1, 1))

    def from_right(v):
        return jnp.where(lane == width - 1, 0.0, pltpu.roll(v, width - 1, 1))

    def shift_x(r, carry):
        v = xraw[r]
        vf = v.astype(jnp.float32)
        xs[r, pl.ds(0, ch), :] = from_left(vf).astype(jnp.bfloat16)
        xs[r, pl.ds(ch, ch), :] = v
        xs[r, pl.ds(2 * ch, ch), :] = from_right(vf).astype(jnp.bfloat16)
        return carry

    local_x.wait()
    lax.fori_loop(1, rows + 1, shift_x, 0)

    for k in range(2):
        across(*edge_rows(k)).wait_recv()
        forward(*edge_rows(k)).start()
    send_halo(2)
    local_g.wait()
    to_sib.wait_recv()
    send_halo(1)
    for k in range(2):
        forward(*edge_rows(k)).wait_recv()
    send_halo(3)

    local_w.wait()
    for p in range(1, 4):
        weights(p).wait_recv()
    for r in range(3):
        block = wall[:, r * 128:(r + 1) * 128].astype(jnp.float32)
        wlhs[:, r * 128:(r + 1) * 128] = block.T[:3 * ch].astype(jnp.bfloat16)

    @pl.when(has_prev)
    def _():
        halo_x(0).wait_recv()

    @pl.when(has_next)
    def _():
        halo_x(1).wait_recv()

    shift_x(0, 0)
    shift_x(rows + 1, 0)

    def filter_row(h, part, acc):
        g = gall[h + 1, part * 2 * ch:(part + 1) * 2 * ch, :]
        v = xs[pl.ds(h, 3)].reshape(9 * ch, width)
        return acc + lax.dot_general(g, v, NT, preferred_element_type=jnp.float32)

    def data_row(h):
        g = gall[pl.ds(h, 3)].reshape(12 * ch, width)
        r = jnp.dot(wlhs[...], g, preferred_element_type=jnp.float32)
        out = r[ch:2 * ch] + from_right(r[:ch]) + from_left(r[2 * ch:])
        out_ref[h] = out.astype(out_ref.dtype)

    q = s // stride
    owner = lax.rem(s, stride) == 0

    def piece_out(part, dest):
        return remote(fs.at[part, dest], rs.at[part, s], rs_s.at[part, dest], rs_r.at[part, s],
                      (dest * stride, f))

    def piece_in(part, src):
        return remote(fs.at[part, 0], rs.at[part, src], rs_s.at[part, 0], rs_r.at[part, src], (s, f))

    def scatter(part, acc):
        fs[part] = acc.reshape(PIECES, 8, 9 * ch)

        def send(i, carry):
            dest = lax.rem(q + i, PIECES)

            @pl.when(dest * stride != s)
            def _():
                piece_out(part, dest).start()

            return carry

        lax.fori_loop(0, PIECES, send, 0)

    def final_out(part, t):
        low = q < PIECES // 2
        home = jnp.where(low, peers[2 * part], peers[2 * part + 1])
        slot = lax.rem(q, PIECES // 2)
        return home, remote(red.at[part], gw_ref.at[f, slot], ag_s.at[part, t],
                            ag_r.at[part, q], (t, home))

    def final_in(part, k):
        src = peers[2 * part + k // (PIECES // 2)]
        slot = k % (PIECES // 2)
        return remote(red.at[part], gw_ref.at[src, slot], ag_s.at[part, 0], ag_r.at[part, k], (s, f))

    def reduce(part):
        @pl.when(owner)
        def _():
            def add(i, acc):
                src = lax.rem(s + i, n)
                piece_in(part, src).wait_recv()
                return acc + rs[part, src]

            red[part] = lax.fori_loop(1, n, add, fs[part, q])

            def send(i, carry):
                t = lax.rem(s + i, n)
                home, copy = final_out(part, t)

                @pl.when(jnp.logical_or(t != s, home != f))
                def _():
                    copy.start()

                return carry

            lax.fori_loop(0, n, send, 0)
            if part == 0:
                @pl.when(q < PIECES // 2)
                def _():
                    gw_ref[f, lax.rem(q, PIECES // 2)] = red[part]

    def finish(part):
        for k in range(PIECES):
            if part == 0 and k < PIECES // 2:
                @pl.when(s != k * stride)
                def _():
                    final_in(part, k).wait_recv()
            else:
                final_in(part, k).wait_recv()

        def sent(i, carry):
            dest = lax.rem(q + i, PIECES)

            @pl.when(dest * stride != s)
            def _():
                piece_out(part, dest).wait_send()

            return carry

        lax.fori_loop(0, PIECES, sent, 0)

        @pl.when(owner)
        def _():
            def sent_final(i, carry):
                t = lax.rem(s + i, n)
                home, copy = final_out(part, t)

                @pl.when(jnp.logical_or(t != s, home != f))
                def _():
                    copy.wait_send()

                return carry

            lax.fori_loop(0, n, sent_final, 0)

    zero = jnp.zeros((2 * ch, 9 * ch), jnp.float32)
    acc = lax.fori_loop(0, rows, lambda h, a: filter_row(h, 0, a), zero)
    scatter(0, acc)

    for p in range(4):
        @pl.when(has_prev)
        def _():
            halo_g(p, 0).wait_recv()

        @pl.when(has_next)
        def _():
            halo_g(p, 1).wait_recv()

    acc = filter_row(0, 1, zero)
    acc = filter_row(rows - 1, 1, acc)

    def arrive(k):
        across(1 + 2 * k, 2, 2 + k).wait_recv()
        forward(1 + 2 * k, 2, 2 + k).start()
        forward(1 + 2 * k, 2, 2 + k).wait_recv()

    def step(k, acc):
        arrive(k)
        acc = filter_row(1 + 2 * k, 1, acc)
        acc = filter_row(2 + 2 * k, 1, acc)
        data_row(2 * k)
        data_row(2 * k + 1)
        return acc

    middle = steps // 2
    acc = lax.fori_loop(0, middle, step, acc)
    reduce(0)
    acc = lax.fori_loop(middle, steps - 1, step, acc)
    arrive(steps - 1)
    acc = filter_row(rows - 3, 1, acc)
    acc = filter_row(rows - 2, 1, acc)
    scatter(1, acc)

    def last(h, carry):
        data_row(h)
        return carry

    lax.fori_loop(rows - 4, rows, last, 0)
    reduce(1)

    for k in range(2):
        across(*edge_rows(k)).wait_send()
        forward(*edge_rows(k)).wait_send()

    def sent_rows(k, carry):
        across(1 + 2 * k, 2, 2 + k).wait_send()
        forward(1 + 2 * k, 2, 2 + k).wait_send()
        return carry

    lax.fori_loop(0, steps, sent_rows, 0)
    to_sib.wait_send()
    for p in range(1, 4):
        weights(p).wait_send()

    @pl.when(has_next)
    def _():
        halo_x(0).wait_send()
        for p in range(4):
            halo_g(p, 0).wait_send()

    @pl.when(has_prev)
    def _():
        halo_x(1).wait_send()
        for p in range(4):
            halo_g(p, 1).wait_send()

    finish(0)
    finish(1)


def on_device(features, grad_out, weight):
    n = lax.axis_size("space")
    rows, ch, width = features.shape
    scale = jnp.sqrt(jnp.float32(rows * n * width))
    w = weight[::-1].reshape(3, 3, ch, 4, ch).transpose(3, 2, 0, 1, 4).reshape(4, ch, 3, 3 * ch)
    w = jnp.pad(w, ((0, 0), (0, 0), (0, 0), (0, 128 - 3 * ch))).reshape(4, ch, 384)
    chunks = 2 + (rows - 2) // 2
    dma = pltpu.SemaphoreType.DMA
    half = PIECES // 2
    flops = 4 * 9 * 4 * ch * ch * rows * width
    grad_features, raw = pl.pallas_call(
        functools.partial(kernel, n, rows, ch, width),
        out_shape=(jax.ShapeDtypeStruct((rows, ch, width), jnp.bfloat16),
                   jax.ShapeDtypeStruct((4, half, 8, 9 * ch), jnp.float32)),
        in_specs=[pl.BlockSpec(memory_space=pl.ANY)] * 3,
        out_specs=(pl.BlockSpec(memory_space=pltpu.VMEM), pl.BlockSpec(memory_space=pltpu.VMEM)),
        scratch_shapes=[
            pltpu.VMEM((rows + 2, 4 * ch, width), jnp.bfloat16),
            pltpu.VMEM((rows + 2, ch, width), jnp.bfloat16),
            pltpu.VMEM((rows + 2, 3 * ch, width), jnp.bfloat16),
            pltpu.VMEM((4 * ch, 384), jnp.bfloat16),
            pltpu.VMEM((3 * ch, 384), jnp.bfloat16),
            pltpu.VMEM((2, PIECES, 8, 9 * ch), jnp.float32),
            pltpu.VMEM((2, n, 8, 9 * ch), jnp.float32),
            pltpu.VMEM((2, 8, 9 * ch), jnp.float32),
            dma((3,)), dma, dma, dma((chunks,)), dma((chunks,)), dma((chunks,)), dma((chunks,)),
            dma((4, 2)), dma((4, 2)), dma((2,)), dma((2,)), dma((4,)), dma((4,)),
            dma((2, PIECES)), dma((2, n)), dma((2, n)), dma((2, PIECES)),
        ],
        compiler_params=pltpu.CompilerParams(
            collective_id=0, has_side_effects=True, vmem_limit_bytes=40 * 1024 * 1024),
        cost_estimate=pl.CostEstimate(flops=flops, bytes_accessed=8 * 1024 * 1024, transcendentals=0),
    )(features, grad_out, w)
    raw = raw.reshape(4, ch, 3, 3, ch).transpose(2, 3, 1, 0, 4).reshape(3, 3, ch, 4 * ch)
    return (grad_features, raw / scale)


def solution(mesh):
    in_specs = (P("space", "filt", None), P("space", "filt", None), P(None, None, "filt", None))
    out_specs = (P("space", "filt", None), P(None, None, "filt", None))
    return jax.shard_map(
        on_device, mesh=mesh, in_specs=in_specs, out_specs=out_specs, check_vma=False
    )
```

```python
import functools

import jax
import jax.numpy as jnp
from jax import lax
from jax.experimental import pallas as pl
from jax.experimental.pallas import tpu as pltpu
from jax.sharding import PartitionSpec as P

MESH = pl.DeviceIdType.MESH
NT = (((1,), (1,)), ((), ()))
PIECES = 8


def kernel(n, rows, ch, width, x_ref, g_ref, w_ref, out_ref, gw_ref,
           gall, xraw, xs, wall, wlhs, fs, rs, red,
           loc, sib_s, sib_r, px_s, px_r, fw_s, fw_r, hg_s, hg_r, hx_s, hx_r,
           w_s, w_r, rs_s, rs_r, ag_s, ag_r):
    s = lax.axis_index("space")
    f = lax.axis_index("filt")
    total = 4 * n
    me = s * 4 + f
    sib = f + 1 - 2 * lax.rem(f, 2)
    far = lax.rem(f + 2, 4)
    diag = lax.rem(sib + 2, 4)
    peers = (f, sib, far, diag)
    stride = n // PIECES
    steps = (rows - 2) // 2

    barrier = pltpu.get_barrier_semaphore()

    def greet(i, carry):
        t = lax.rem(me + i, total)
        pl.semaphore_signal(barrier, inc=1, device_id=(t // 4, lax.rem(t, 4)), device_id_type=MESH)
        return carry

    lax.fori_loop(1, total, greet, 0)

    local_g = pltpu.make_async_copy(g_ref, gall.at[pl.ds(1, rows), pl.ds(0, ch)], loc.at[0])
    local_x = pltpu.make_async_copy(x_ref, xraw.at[pl.ds(1, rows)], loc.at[1])
    local_w = pltpu.make_async_copy(w_ref.at[f], wall.at[pl.ds(0, ch)], loc.at[2])
    local_g.start()
    local_x.start()
    local_w.start()
    pl.semaphore_wait(barrier, total - 1)

    def remote(src, dst, ssem, rsem, dev):
        return pltpu.make_async_remote_copy(
            src_ref=src, dst_ref=dst, send_sem=ssem, recv_sem=rsem,
            device_id=dev, device_id_type=MESH)

    def across(first, count, c):
        return remote(g_ref.at[pl.ds(first, count)],
                      gall.at[pl.ds(first + 1, count), pl.ds(2 * ch, ch)],
                      px_s.at[c], px_r.at[c], (s, far))

    def forward(first, count, c):
        return remote(gall.at[pl.ds(first + 1, count), pl.ds(2 * ch, ch)],
                      gall.at[pl.ds(first + 1, count), pl.ds(3 * ch, ch)],
                      fw_s.at[c], fw_r.at[c], (s, sib))

    def edge_rows(k):
        return (0 if k == 0 else rows - 1, 1, k)

    def weights(p):
        return remote(w_ref.at[peers[p]], wall.at[pl.ds(p * ch, ch)], w_s.at[p], w_r.at[p],
                      (s, peers[p]))

    to_sib = remote(g_ref, gall.at[pl.ds(1, rows), pl.ds(ch, ch)], sib_s, sib_r, (s, sib))

    def halo_g(p, d):
        part = pl.ds(p * ch, ch)
        src = gall.at[rows if d == 0 else 1, part] if p else g_ref.at[rows - 1 if d == 0 else 0]
        return remote(src, gall.at[0 if d == 0 else rows + 1, part],
                      hg_s.at[p, d], hg_r.at[p, d], (s + 1 if d == 0 else s - 1, f))

    def halo_x(d):
        return remote(x_ref.at[rows - 1 if d == 0 else 0], xraw.at[0 if d == 0 else rows + 1],
                      hx_s.at[d], hx_r.at[d], (s + 1 if d == 0 else s - 1, f))

    has_next = s < n - 1
    has_prev = s > 0

    def share_halo(p, d):
        row = 0 if d == 0 else rows + 1
        return remote(gall.at[row, pl.ds(p * ch, ch)], gall.at[row, pl.ds((p + 1) * ch, ch)],
                      hg_s.at[p + 1, d], hg_r.at[p + 1, d], (s, sib))

    def pass_halo(p):
        @pl.when(has_prev)
        def _():
            halo_g(p, 0).wait_recv()
            share_halo(p, 0).start()

        @pl.when(has_next)
        def _():
            halo_g(p, 1).wait_recv()
            share_halo(p, 1).start()

    def send_halo(p):
        @pl.when(has_next)
        def _():
            halo_g(p, 0).start()

        @pl.when(has_prev)
        def _():
            halo_g(p, 1).start()

    across(*edge_rows(0)).start()
    across(*edge_rows(1)).start()
    for p in (2, 3, 1):
        weights(p).start()

    def start_across(k, carry):
        across(1 + 2 * k, 2, 2 + k).start()
        return carry

    lax.fori_loop(0, steps, start_across, 0)
    to_sib.start()

    @pl.when(has_next)
    def _():
        halo_x(0).start()

    @pl.when(has_prev)
    def _():
        halo_x(1).start()

    send_halo(0)

    @pl.when(jnp.logical_not(has_prev))
    def _():
        gall[0] = jnp.zeros(gall.shape[1:], gall.dtype)
        xraw[0] = jnp.zeros(xraw.shape[1:], xraw.dtype)

    @pl.when(jnp.logical_not(has_next))
    def _():
        gall[rows + 1] = jnp.zeros(gall.shape[1:], gall.dtype)
        xraw[rows + 1] = jnp.zeros(xraw.shape[1:], xraw.dtype)

    lane = lax.broadcasted_iota(jnp.int32, (ch, width), 1)

    def from_left(v):
        return jnp.where(lane == 0, 0.0, pltpu.roll(v, 1, 1))

    def from_right(v):
        return jnp.where(lane == width - 1, 0.0, pltpu.roll(v, width - 1, 1))

    def shift_x(r, carry):
        v = xraw[r]
        vf = v.astype(jnp.float32)
        xs[r, pl.ds(0, ch), :] = from_left(vf).astype(jnp.bfloat16)
        xs[r, pl.ds(ch, ch), :] = v
        xs[r, pl.ds(2 * ch, ch), :] = from_right(vf).astype(jnp.bfloat16)
        return carry

    local_x.wait()
    lax.fori_loop(1, rows + 1, shift_x, 0)

    for k in range(2):
        across(*edge_rows(k)).wait_recv()
        forward(*edge_rows(k)).start()
    send_halo(2)
    local_g.wait()
    to_sib.wait_recv()
    local_w.wait()
    for p in range(1, 4):
        weights(p).wait_recv()
    for r in range(3):
        block = wall[:, (2 - r) * 128:(3 - r) * 128].astype(jnp.float32)
        wlhs[:, r * 128:(r + 1) * 128] = block.T[:3 * ch].astype(jnp.bfloat16)

    @pl.when(has_prev)
    def _():
        halo_x(0).wait_recv()

    @pl.when(has_next)
    def _():
        halo_x(1).wait_recv()

    shift_x(0, 0)
    shift_x(rows + 1, 0)

    def filter_row(h, part, acc):
        g = gall[h + 1, part * 2 * ch:(part + 1) * 2 * ch, :]
        v = xs[pl.ds(h, 3)].reshape(9 * ch, width)
        return acc + lax.dot_general(g, v, NT, preferred_element_type=jnp.float32)

    def data_row(h):
        g = gall[pl.ds(h, 3)].reshape(12 * ch, width)
        r = jnp.dot(wlhs[...], g, preferred_element_type=jnp.float32)
        out = r[ch:2 * ch] + from_right(r[:ch]) + from_left(r[2 * ch:])
        out_ref[h] = out.astype(out_ref.dtype)

    q = s // stride
    owner = lax.rem(s, stride) == 0

    def piece_out(part, dest):
        return remote(fs.at[part, dest], rs.at[part, s], rs_s.at[part, dest], rs_r.at[part, s],
                      (dest * stride, f))

    def piece_in(part, src):
        return remote(fs.at[part, 0], rs.at[part, src], rs_s.at[part, 0], rs_r.at[part, src], (s, f))

    def scatter(part, acc):
        fs[part] = acc.reshape(PIECES, 8, 9 * ch)

        def send(i, carry):
            dest = lax.rem(q + i, PIECES)

            @pl.when(dest * stride != s)
            def _():
                piece_out(part, dest).start()

            return carry

        lax.fori_loop(0, PIECES, send, 0)

    def final_out(part, t):
        low = q < PIECES // 2
        home = jnp.where(low, peers[2 * part], peers[2 * part + 1])
        slot = lax.rem(q, PIECES // 2)
        return home, remote(red.at[part], gw_ref.at[f, slot], ag_s.at[part, t],
                            ag_r.at[part, q], (t, home))

    def final_in(part, k):
        src = peers[2 * part + k // (PIECES // 2)]
        slot = k % (PIECES // 2)
        return remote(red.at[part], gw_ref.at[src, slot], ag_s.at[part, 0], ag_r.at[part, k], (s, f))

    def reduce(part):
        @pl.when(owner)
        def _():
            def add(i, acc):
                src = lax.rem(s + i, n)
                piece_in(part, src).wait_recv()
                return acc + rs[part, src]

            red[part] = lax.fori_loop(1, n, add, fs[part, q])

            def send(i, carry):
                t = lax.rem(s + i, n)
                home, copy = final_out(part, t)

                @pl.when(jnp.logical_or(t != s, home != f))
                def _():
                    copy.start()

                return carry

            lax.fori_loop(0, n, send, 0)
            if part == 0:
                @pl.when(q < PIECES // 2)
                def _():
                    gw_ref[f, lax.rem(q, PIECES // 2)] = red[part]

    def finish(part):
        for k in range(PIECES):
            if part == 0 and k < PIECES // 2:
                @pl.when(s != k * stride)
                def _():
                    final_in(part, k).wait_recv()
            else:
                final_in(part, k).wait_recv()

        def sent(i, carry):
            dest = lax.rem(q + i, PIECES)

            @pl.when(dest * stride != s)
            def _():
                piece_out(part, dest).wait_send()

            return carry

        lax.fori_loop(0, PIECES, sent, 0)

        @pl.when(owner)
        def _():
            def sent_final(i, carry):
                t = lax.rem(s + i, n)
                home, copy = final_out(part, t)

                @pl.when(jnp.logical_or(t != s, home != f))
                def _():
                    copy.wait_send()

                return carry

            lax.fori_loop(0, n, sent_final, 0)

    zero = jnp.zeros((2 * ch, 9 * ch), jnp.float32)
    acc = lax.fori_loop(0, rows, lambda h, a: filter_row(h, 0, a), zero)
    scatter(0, acc)
    pass_halo(0)

    def arrive(k):
        across(1 + 2 * k, 2, 2 + k).wait_recv()
        forward(1 + 2 * k, 2, 2 + k).start()

    def arrive_far(k):
        forward(1 + 2 * k, 2, 2 + k).wait_recv()

    for k in range(2):
        forward(*edge_rows(k)).wait_recv()
    acc = filter_row(0, 1, zero)
    acc = filter_row(rows - 1, 1, acc)

    def step(k, acc):
        arrive(k)
        arrive_far(k - 1)
        acc = filter_row(2 * k - 1, 1, acc)
        acc = filter_row(2 * k, 1, acc)

        @pl.when(k > 1)
        def _():
            data_row(2 * k - 2)

        data_row(2 * k - 1)
        return acc

    middle = (steps + 1) // 2
    arrive(0)
    acc = lax.fori_loop(1, middle, step, acc)
    pass_halo(2)
    reduce(0)
    acc = lax.fori_loop(middle, steps, step, acc)
    arrive_far(steps - 1)
    acc = filter_row(rows - 3, 1, acc)
    acc = filter_row(rows - 2, 1, acc)
    scatter(1, acc)

    def last(h, carry):
        data_row(h)
        return carry

    lax.fori_loop(rows - 4, rows - 1, last, 0)
    for p in (0, 2):
        @pl.when(has_prev)
        def _():
            share_halo(p, 0).wait_recv()

        @pl.when(has_next)
        def _():
            share_halo(p, 1).wait_recv()

    data_row(0)
    data_row(rows - 1)
    reduce(1)

    for k in range(2):
        across(*edge_rows(k)).wait_send()
        forward(*edge_rows(k)).wait_send()

    def sent_rows(k, carry):
        across(1 + 2 * k, 2, 2 + k).wait_send()
        forward(1 + 2 * k, 2, 2 + k).wait_send()
        return carry

    lax.fori_loop(0, steps, sent_rows, 0)
    to_sib.wait_send()
    for p in range(1, 4):
        weights(p).wait_send()

    @pl.when(has_next)
    def _():
        halo_x(0).wait_send()
        for p in (0, 2):
            halo_g(p, 0).wait_send()
            share_halo(p, 1).wait_send()

    @pl.when(has_prev)
    def _():
        halo_x(1).wait_send()
        for p in (0, 2):
            halo_g(p, 1).wait_send()
            share_halo(p, 0).wait_send()

    finish(0)
    finish(1)


def on_device(features, grad_out, weight):
    n = lax.axis_size("space")
    rows, ch, width = features.shape
    scale = jnp.sqrt(jnp.float32(rows * n * width))
    w = weight.reshape(3, 3, ch, 4, ch).transpose(3, 2, 0, 1, 4).reshape(4, ch, 3, 3 * ch)
    w = jnp.pad(w, ((0, 0), (0, 0), (0, 0), (0, 128 - 3 * ch))).reshape(4, ch, 384)
    chunks = 2 + (rows - 2) // 2
    dma = pltpu.SemaphoreType.DMA
    half = PIECES // 2
    flops = 4 * 9 * 4 * ch * ch * rows * width
    grad_features, raw = pl.pallas_call(
        functools.partial(kernel, n, rows, ch, width),
        out_shape=(jax.ShapeDtypeStruct((rows, ch, width), jnp.bfloat16),
                   jax.ShapeDtypeStruct((4, half, 8, 9 * ch), jnp.float32)),
        in_specs=[pl.BlockSpec(memory_space=pl.ANY)] * 3,
        out_specs=(pl.BlockSpec(memory_space=pltpu.VMEM), pl.BlockSpec(memory_space=pltpu.VMEM)),
        scratch_shapes=[
            pltpu.VMEM((rows + 2, 4 * ch, width), jnp.bfloat16),
            pltpu.VMEM((rows + 2, ch, width), jnp.bfloat16),
            pltpu.VMEM((rows + 2, 3 * ch, width), jnp.bfloat16),
            pltpu.VMEM((4 * ch, 384), jnp.bfloat16),
            pltpu.VMEM((3 * ch, 384), jnp.bfloat16),
            pltpu.VMEM((2, PIECES, 8, 9 * ch), jnp.float32),
            pltpu.VMEM((2, n, 8, 9 * ch), jnp.float32),
            pltpu.VMEM((2, 8, 9 * ch), jnp.float32),
            dma((3,)), dma, dma, dma((chunks,)), dma((chunks,)), dma((chunks,)), dma((chunks,)),
            dma((4, 2)), dma((4, 2)), dma((2,)), dma((2,)), dma((4,)), dma((4,)),
            dma((2, PIECES)), dma((2, n)), dma((2, n)), dma((2, PIECES)),
        ],
        compiler_params=pltpu.CompilerParams(
            collective_id=0, has_side_effects=True, vmem_limit_bytes=40 * 1024 * 1024),
        cost_estimate=pl.CostEstimate(flops=flops, bytes_accessed=8 * 1024 * 1024, transcendentals=0),
    )(features, grad_out, w)
    raw = raw.reshape(4, ch, 3, 3, ch).transpose(2, 3, 1, 0, 4).reshape(3, 3, ch, 4 * ch)
    return (grad_features, raw / scale)


def solution(mesh):
    in_specs = (P("space", "filt", None), P("space", "filt", None), P(None, None, "filt", None))
    out_specs = (P("space", "filt", None), P(None, None, "filt", None))
    return jax.shard_map(
        on_device, mesh=mesh, in_specs=in_specs, out_specs=out_specs, check_vma=False
    )
```
